32 devices in a mesh: seq: 8 (over z, y), dp: 4 (over x, core).
Axes of the slice: x: 2, y: 2, z: 4, core: 2. Of those that a mesh axis runs over, the one named last changes fastest.
Arguments:
- tokens: int32 [4, 1024], P('dp', 'seq'), may hold values from 65 to 116, as said below
- embed: bfloat16 [512, 1536], replicated, may hold values from -6 to 6
- taps: float32 [3, 3, 512], replicated, may hold values from -3.5 to 3.5
- skip: float32 [512], replicated, may hold values from -4 to 4
- rates: float32 [512], replicated, may hold values from 0.3 to 34
- w_one: float32 [128, 128], replicated, may hold values from -0.5 to 0.5
- b_one: float32 [128], replicated, may hold values from -4 to 4
- w_two: float32 [128, 128], replicated, may hold values from -0.5 to 0.5
- b_two: float32 [128], replicated, may hold values from -4 to 4
- w_three: float32 [128, 512], replicated, may hold values from -0.5 to 0.5
- cotangent: bfloat16 [4, 1024, 512], P('dp', 'seq'), may hold values from -0.029907227 to 0.029907227
Outputs:
- gated: bfloat16 [4, 1024, 512], P('dp', 'seq')
- grad_w_one: float32 [128, 128], replicated
- grad_b_one: float32 [128], replicated
- grad_w_two: float32 [128, 128], replicated
- grad_b_two: float32 [128], replicated
- grad_w_three: float32 [128, 512], replicated
The draws below stay inside these ranges and needn't reach their ends.
Inputs may be any that keep to these rules, and one draw needn't show every extreme that they name: `tokens`: byte codes of the letters A, C, G, T, their lower-case forms, N and n.
All inputs are finite; a program needn't handle non-finite values.
Results may differ from the reference program's by a relative error of at most 0.001.
Values sent between devices are 32-bit elements; how exact they have to be, the bound alone decides.
No kernel may reach another device: no remote copies, remote signals or barrier semaphores. Data moves between devices by JAX's collectives and lax.ppermute only.
A program may use at most 64 MiB of HBM per device.

```python
import math
import jax
import jax.numpy as jnp
from jax import lax

CHANNELS = 512
VOCAB = 512
ORDER = 128
FEATURES = 128
SHORT = 3
LENGTH = 1024
BATCH = 4


def draw_tokens(key, part):
    base_codes = jnp.array([65, 67, 71, 84, 97, 99, 103, 116, 78, 110], dtype=jnp.int32)
    letter_index = jax.random.randint(key, (BATCH, LENGTH), 0, 10)
    return base_codes[letter_index]


def draw_rates(key, part):
    key_slow = jax.random.fold_in(key, 0)
    top_rate = float(LENGTH // 30)
    drawn = jnp.exp(jax.random.uniform(key_slow, (CHANNELS,), jnp.float32, math.log(0.5), math.log(top_rate)))
    return jnp.clip(drawn, 0.3, top_rate)


def block_levels(rng, dims, cuts, smallest, largest):
    loudness, own = 1.0, jax.random.fold_in(rng, 6)
    for axis_at, blocks in cuts:
        steps = jnp.exp(jax.random.uniform(jax.random.fold_in(own, axis_at), (blocks,), jnp.float32, smallest / len(cuts), largest / len(cuts)))
        loudness = loudness * jnp.repeat(steps, dims[axis_at] // blocks).reshape([-1 if axis == axis_at else 1 for axis in range(len(dims))])
    return loudness


def centred(rng, extent, deviation, bound, pieces=(), kind=jnp.bfloat16):
    gain = block_levels(rng, extent, pieces, -0.22, 0.18) if pieces else 1.0
    values = jax.random.normal(rng, extent, jnp.float32) * deviation * gain
    return jnp.minimum(jnp.maximum(values, -bound), bound).astype(kind)


def setup_inputs(seed: int = 0) -> dict:
    streams_of = jax.random.split(jax.random.key(seed), 12)
    return {
        "tokens": draw_tokens(jax.random.fold_in(streams_of[11], 71), 0),
        "embed": centred(streams_of[1], (VOCAB, 3 * CHANNELS), 1.0, 6.0),
        "taps": centred(streams_of[2], (3, SHORT, CHANNELS), SHORT ** -0.5, 3.5, (), jnp.float32),
        "skip": centred(streams_of[3], (CHANNELS,), 1.0, 4.0, (), jnp.float32),
        "rates": draw_rates(jax.random.fold_in(streams_of[11], 71), 0),
        "w_one": centred(streams_of[5], (FEATURES, ORDER), FEATURES ** -0.5, 0.5, (), jnp.float32),
        "b_one": centred(streams_of[6], (ORDER,), 1.0, 4.0, (), jnp.float32),
        "w_two": centred(streams_of[7], (ORDER, ORDER), ORDER ** -0.5, 0.5, (), jnp.float32),
        "b_two": centred(streams_of[8], (ORDER,), 1.0, 4.0, (), jnp.float32),
        "w_three": centred(streams_of[9], (ORDER, CHANNELS), ORDER ** -0.5, 0.5, (), jnp.float32),
        "cotangent": centred(streams_of[10], (BATCH, LENGTH, CHANNELS), 0.005, 0.029907227, ((0, 4), (1, 8))),
    }


full_turn = 2.0 * math.pi

def band_numbers(length, band_count):
    return [max(band_index + 1, int(0.4 * length ** (band_index / (band_count - 1)))) for band_index in range(band_count)]

def position_features(positions, length, band_count):
    numbers = jnp.array(band_numbers(length, band_count), dtype=jnp.int32)
    upper_part = positions[:, None] // 256
    lower_part = positions[:, None] % 256
    wrapped = 256 * numbers[None, :] % length
    residue = (upper_part * wrapped % length + lower_part * numbers[None, :]) % length
    angles = residue.astype(jnp.float32) * (full_turn / length)
    return jnp.concatenate([jnp.sin(angles), jnp.cos(angles)], axis=1)

def matmul(left, right):
    return jnp.dot(left, right, precision=lax.Precision.HIGHEST, preferred_element_type=jnp.float32)

def featurize(tokens_row, embed, taps):
    reach = taps.shape[1] - 1
    chan_count = taps.shape[2]
    length = tokens_row.shape[0]
    looked = jnp.take(embed, tokens_row, axis=0).astype(jnp.float32)
    padded = jnp.concatenate([jnp.zeros((reach, looked.shape[1]), jnp.float32), looked], axis=0)
    outputs = []
    for branch_index in range(3):
        total = jnp.zeros((length, chan_count), jnp.float32)
        for tap_index in range(reach + 1):
            begin = reach - tap_index
            total = total + taps[branch_index, tap_index][None, :] * padded[begin:begin + length, branch_index * chan_count:(branch_index + 1) * chan_count]
        outputs.append(total)
    return (outputs[0], outputs[1], outputs[2])

def reference(tokens, embed, taps, skip, rates, w_one, b_one, w_two, b_two, w_three, cotangent):
    positions = jnp.arange(LENGTH, dtype=jnp.int32)
    features = position_features(positions, LENGTH, FEATURES // 2)
    pre_one = matmul(features, w_one) + b_one
    act_one = jnp.sin(pre_one)
    pre_two = matmul(act_one, w_two) + b_two
    act_two = jnp.sin(pre_two)
    window = jnp.exp(-rates[None, :] * (positions.astype(jnp.float32) / LENGTH)[:, None]) * (1.0 / math.sqrt(LENGTH))
    filter_taps = matmul(act_two, w_three) * window
    period = 2 * LENGTH
    spectrum_taps = jnp.fft.rfft(filter_taps, n=period, axis=0)
    gated_rows = []
    lag_total = jnp.zeros((LENGTH, CHANNELS), jnp.float32)
    for seq_index in range(BATCH):
        query, keyed, valued = featurize(tokens[seq_index], embed, taps)
        signal = keyed * valued
        spectrum_signal = jnp.fft.rfft(signal, n=period, axis=0)
        convolved = jnp.fft.irfft(spectrum_signal * spectrum_taps, n=period, axis=0)[:LENGTH]
        gated_rows.append((query * (convolved + skip[None, :] * signal)).astype(jnp.bfloat16))
        upstream = cotangent[seq_index].astype(jnp.float32) * query
        spectrum_up = jnp.fft.rfft(upstream, n=period, axis=0)
        lag_total = lag_total + jnp.fft.irfft(jnp.conj(spectrum_signal) * spectrum_up, n=period, axis=0)[:LENGTH]
    slopes = lag_total * window
    grad_three = matmul(act_two.T, slopes)
    back_two = matmul(slopes, w_three.T) * jnp.cos(pre_two)
    grad_two = matmul(act_one.T, back_two)
    bias_two = lax.optimization_barrier(jnp.sum(back_two, axis=0))
    back_one = matmul(back_two, w_two.T) * jnp.cos(pre_one)
    grad_one = matmul(features.T, back_one)
    bias_one = lax.optimization_barrier(jnp.sum(back_one, axis=0))
    return (jnp.stack(gated_rows), grad_one, bias_one, grad_two, bias_two, grad_three)
```

```python
import functools
import math

import jax
import jax.numpy as jnp
import ml_dtypes
import numpy as np
from jax import lax
from jax.experimental import pallas as pl
from jax.experimental.pallas import tpu as pltpu
from jax.sharding import PartitionSpec as P

LETTERS = (65, 67, 71, 84, 97, 99, 103, 116, 78, 110)
GROUP = 16
LANES = 128
CHUNK = 8
VMEM = 56 * 1024 * 1024
F32 = jnp.float32
BF16 = jnp.bfloat16


def halves(table):
    high = table.astype(np.float32).astype(ml_dtypes.bfloat16)
    low = (table - high.astype(np.float64)).astype(np.float32).astype(ml_dtypes.bfloat16)
    return high, low


def band_numbers(length, band_count):
    return [
        max(band + 1, int(0.4 * length ** (band / (band_count - 1)))) for band in range(band_count)
    ]


@functools.cache
def feature_tables(length, band_count):
    numbers = np.array(band_numbers(length, band_count), np.int64)
    residue = (numbers[:, None] * np.arange(length, dtype=np.int64)[None, :]) % length
    angles = residue * (2.0 * math.pi / length)
    return halves(np.concatenate([np.sin(angles), np.cos(angles)], axis=0))


@functools.cache
def transform_tables(rows):
    theta = np.pi * (np.arange(rows) + 0.5) / rows
    angles = np.arange(rows)[:, None] * theta[None, :]
    forward = np.concatenate([np.cos(angles), -np.sin(angles)], axis=1)
    high, low = halves(forward)
    first = np.concatenate([high, low], axis=0)
    inv_high, inv_low = halves(forward.T / rows)
    inverse = np.concatenate([inv_high, inv_low], axis=1)
    sign = np.broadcast_to(np.where(np.arange(rows) % 2 == 0, 1.0, -1.0), (8, rows))
    return first, inverse, sign.astype(np.float32)


@functools.cache
def letter_tables(lanes):
    code = np.full((lanes,), -1, np.int32)
    pick = np.zeros((lanes, lanes), np.float32)
    for row in range(6 * GROUP):
        if row % GROUP < len(LETTERS):
            code[row] = LETTERS[row % GROUP]
            pick[row, code[row]] = 1.0
    code = np.ascontiguousarray(np.broadcast_to(code[:, None], (lanes, lanes)))
    return code, pick.astype(ml_dtypes.bfloat16)


def split(x):
    high = x.astype(BF16)
    return high, (x - high.astype(F32)).astype(BF16)


def mm(a, b, ca=1, cb=0):
    return lax.dot_general(a, b, (((ca,), (cb,)), ((), ())), preferred_element_type=F32)


def left_mm(stack, high, low, cb=0):
    m = stack.shape[0] // 2
    both = mm(stack, high, cb=cb)
    return both[:m] + both[m:] + mm(stack[:m], low, cb=cb)


def sin_cos(x):
    turns = jnp.floor(x * (2.0 / math.pi) + 0.5)
    r = x - turns * 1.5703125
    r = r - turns * 4.837512969970703125e-4
    r = r - turns * 7.549789948768648e-8
    quarter = turns.astype(jnp.int32)
    z = r * r
    s = r + r * z * (-1.6666654611e-1 + z * (8.3321608736e-3 + z * -1.9515295891e-4))
    c = 1.0 + z * (
        -0.5 + z * (4.166664568298827e-2 + z * (-1.388731625493765e-3 + z * 2.443315711809948e-5))
    )
    swap = (quarter & 1) == 1
    sine = jnp.where(swap, c, s)
    cosine = jnp.where(swap, s, c)
    sine = jnp.where((quarter & 2) == 2, -sine, sine)
    cosine = jnp.where(((quarter + 1) & 2) == 2, -cosine, cosine)
    return sine, cosine


def forward(block, first_ref):
    rows = block.shape[1]
    high, low = split(block)
    return mm(jnp.concatenate([high, high], axis=1), first_ref[...]) + mm(low, first_ref[:rows, :])


def inverse(real, imag, inverse_ref):
    rows = real.shape[1]
    high, low = split(jnp.concatenate([real, imag], axis=1))
    both = mm(high, inverse_ref[...])
    return both[:, :rows] + both[:, rows:] + mm(low, inverse_ref[:, :rows])


def window_block(rates, start, rows, length):
    place = (lax.broadcasted_iota(jnp.int32, (1, rows), 1) + start).astype(F32) * (-1.0 / length)
    return jnp.exp(rates * place) * (1.0 / math.sqrt(length))


def prepare(w_one, w_two, w_three, b_one, b_two, order):
    one = jnp.concatenate(split(w_one.T), axis=0)
    two = jnp.concatenate(split(w_two.T), axis=0)
    three = jnp.concatenate(split(w_three.T), axis=0)
    col_one = jnp.broadcast_to(b_one, (order, order)).T
    col_two = jnp.broadcast_to(b_two, (order, order)).T
    return one, two, three, col_one, col_two


def network(feat_high, feat_low, one, two, col_one, col_two):
    count = feat_high.shape[1] // LANES
    act_one, cos_one = sin_cos(
        left_mm(one, feat_high, feat_low) + jnp.concatenate([col_one] * count, axis=1)
    )
    one_high, one_low = split(act_one)
    act_two, cos_two = sin_cos(
        left_mm(two, one_high, one_low) + jnp.concatenate([col_two] * count, axis=1)
    )
    two_high, two_low = split(act_two)
    return one_high, one_low, cos_one, two_high, two_low, cos_two


def lookup_table(embed, taps, pick):
    chosen = mm(pick, embed)
    channels = taps.shape[2]
    pieces = []
    for branch in range(3):
        part = chosen[:, branch * channels : (branch + 1) * channels]
        scaled = [
            part[tap * GROUP : (tap + 1) * GROUP] * taps[branch, tap : tap + 1, :]
            for tap in range(3)
        ]
        high = jnp.concatenate(scaled, axis=0)
        rounded = high.astype(BF16).astype(F32)
        rest = jnp.zeros((LANES - 6 * GROUP, channels), F32)
        pieces.append(jnp.concatenate([rounded, high - rounded, rest], axis=0).T)
    return jnp.concatenate(pieces, axis=0).astype(BF16)


def one_hot(tok_ref, block, code):
    rows = tok_ref.shape[1]

    def row(j):
        got = tok_ref[pl.ds(jnp.maximum(j, 0), 1), :]
        return jnp.where(j >= 0, got, 0)

    now = jnp.broadcast_to(row(block), (8, rows))
    before = jnp.broadcast_to(row(block - 1), (8, rows))
    lane = lax.broadcasted_iota(jnp.int32, (8, rows), 1)
    shifted = [now]
    for tap in (1, 2):
        shifted.append(
            jnp.where(lane < tap, pltpu.roll(before, tap, 1), pltpu.roll(now, tap, 1))
        )
    wide = [jnp.concatenate([s, s], axis=0) for s in shifted]
    rest = jnp.zeros((LANES - 6 * GROUP, rows), jnp.int32)
    spread = jnp.concatenate(wide + wide + [rest], axis=0)
    return jnp.where(spread == code, 1.0, 0.0).astype(BF16)


def pre_kernel(
    length, apart, *refs
):
    (embed, taps, pick, rates, skip, cot, w_one, b_one, w_two, b_two, w_three) = refs[:11]
    refs = refs[11:]
    if not apart:
        feat_high, feat_low, first = refs[:3]
        refs = refs[3:]
    table, rates_col, skip_col, cot_t = refs[:4]
    channels = cot.shape[1]
    table[...] = lookup_table(embed[...], taps[...], pick[...])
    rates_col[...] = jnp.broadcast_to(rates[...], (LANES, channels)).T
    skip_col[...] = jnp.broadcast_to(skip[...], (LANES, channels)).T
    cot_t[...] = cot[...].astype(F32).T
    if not apart:
        one_high, one_low, cos_one, two_high, two_low, cos_two, spectra = refs[4:]
        order = w_one.shape[1]
        one, two, three, col_one, col_two = prepare(
            w_one[...], w_two[...], w_three[...], b_one[...], b_two[...], order
        )
        made = network(feat_high[...], feat_low[...], one, two, col_one, col_two)
        for ref, value in zip((one_high, one_low, cos_one, two_high, two_low, cos_two), made):
            ref[...] = value
        for k in range(length // LANES):
            at = slice(k * LANES, (k + 1) * LANES)
            filt = left_mm(three, two_high[:, at], two_low[:, at]) * window_block(
                rates_col[...], k * LANES, LANES, length
            )
            spectra[k] = forward(filt, first)


def main_kernel(length, apart, *refs):
    (place, tok, code, first, inv, sign, table, rates_col, cot_t) = refs[:9]
    (w_two, w_three, feat_high, feat_low) = refs[9:13]
    refs = refs[13:]
    if apart:
        w_one, b_one, b_two = refs[:3]
        refs = refs[3:]
    else:
        one_high, one_low, cos_one, two_high, two_low, cos_two, spectra = refs[:7]
        refs = refs[7:]
    keep, send, mixed, query_t, signal_t = refs[:5]
    hot, spec, slope_high, slope_low, packed = refs[5:10]
    blocks, rows = tok.shape
    channels = cot_t.shape[0]
    order = w_two.shape[0]
    count = min(blocks, CHUNK)
    chunks = blocks // count
    own = place[0]
    bit = place[1]
    codes = code[...]
    signs = jnp.broadcast_to(sign[0:1, :], (channels, rows))

    three_split = split(w_three[...])
    three_stack = jnp.concatenate(three_split, axis=0)
    two_stack = jnp.concatenate(split(w_two[...]), axis=0)
    if apart:
        one_t, two_t, three_t, col_one, col_two = prepare(
            w_one[...], w_two[...], w_three[...], b_one[...], b_two[...], order
        )

    own_hot = one_hot(tok, own, codes)
    query = mm(table[:channels, :], own_hot)
    query_t[...] = query
    up = forward(cot_t[...] * query, first)
    up_real, up_imag = up[:, :rows], up[:, rows:]
    packed[...] = jnp.zeros(packed.shape, F32)

    def chunk(base):
        static = isinstance(base, int)
        slots = count if static else count + 1
        lane0 = base * rows if static else pl.multiple_of(base * rows, rows * count)
        for i in range(slots):
            hot[:, i * rows : (i + 1) * rows] = one_hot(tok, own - base - i, codes)
        span = pl.ds(lane0, count * rows)
        if apart:
            act_one_high, act_one_low, cosine_one, act_two_high, act_two_low, cosine_two = network(
                feat_high[:, span], feat_low[:, span], one_t, two_t, col_one, col_two
            )
        else:
            act_one_high, act_one_low, cosine_one, act_two_high, act_two_low, cosine_two = (
                r[:, span] for r in (one_high, one_low, cos_one, two_high, two_low, cos_two)
            )
        for i in range(slots):
            both = mm(table[channels:, :], hot[:, i * rows : (i + 1) * rows])
            signal = both[:channels] * both[channels:]
            if i == 0:
                if static:
                    signal_t[...] = signal
                else:

                    @pl.when(base == 0)
                    def _():
                        signal_t[...] = signal

            spec[i] = forward(signal, first)
        for i in range(count):
            real, imag = spec[i, :, :rows], spec[i, :, rows:]
            if i + 1 < slots:
                real = real - signs * spec[i + 1, :, rows:]
                imag = imag + signs * spec[i + 1, :, :rows]
            weight = window_block(rates_col[...], lane0 + i * rows, rows, length)
            if apart:
                at = slice(i * rows, (i + 1) * rows)
                filt = left_mm(three_t, act_two_high[:, at], act_two_low[:, at]) * weight
                got = forward(filt, first)
            else:
                got = spectra[base + i]
            g_real, g_imag = got[:, :rows], got[:, rows:]
            add_real = g_real * real - g_imag * imag
            add_imag = g_real * imag + g_imag * real
            if static and i == 0:
                mixed[:, :rows] = add_real
                mixed[:, rows:] = add_imag
            else:
                mixed[:, :rows] += add_real
                mixed[:, rows:] += add_imag
            lag = inverse(
                up_real * real + up_imag * imag, up_imag * real - up_real * imag, inv
            )
            high, low = split(lag * weight)
            slope_high[:, i * rows : (i + 1) * rows] = high
            slope_low[:, i * rows : (i + 1) * rows] = low

        slopes_high, slopes_low = slope_high[...], slope_low[...]
        grad_three = left_mm(
            jnp.concatenate([act_two_high, act_two_low], axis=0), slopes_high, slopes_low, cb=1
        )
        for slab in range(channels // LANES):
            packed[slab * order : (slab + 1) * order, :] += grad_three[
                :, slab * LANES : (slab + 1) * LANES
            ]
        back_two = left_mm(three_stack, slopes_high, slopes_low) * cosine_two
        two_back = split(back_two)
        grad_two = left_mm(
            jnp.concatenate([act_one_high, act_one_low], axis=0), *two_back, cb=1
        )
        back_one = left_mm(two_stack, *two_back) * cosine_one
        one_back = split(back_one)
        grad_one = left_mm(
            jnp.concatenate([feat_high[:, span], feat_low[:, span]], axis=0), *one_back, cb=1
        )
        ones = jnp.ones((8, count * rows), BF16)
        bias_one = mm(ones, one_back[0], cb=1) + mm(ones, one_back[1], cb=1)
        bias_two = mm(ones, two_back[0], cb=1) + mm(ones, two_back[1], cb=1)
        at = channels // LANES * order
        features = feat_high.shape[0]
        packed[at : at + features, :] += grad_one
        packed[at + features : at + features + order, :] += grad_two
        at = at + features + order
        packed[at : at + 8, :] += bias_one
        packed[at + 8 : at + 16, :] += bias_two

    if chunks == 1:
        chunk(0)
    else:
        mixed[...] = jnp.zeros(mixed.shape, F32)

        @pl.loop(0, chunks)
        def _(q):
            chunk(q * count)

    half = keep.shape[0]
    keep[...] = packed[pl.ds(pl.multiple_of(bit * half, 8), half), :]
    send[...] = packed[pl.ds(pl.multiple_of((1 - bit) * half, 8), half), :]


def gate_kernel(mixed, inv, query_t, signal_t, skip_col, out):
    rows = query_t.shape[1]
    convolved = inverse(mixed[:, :rows], mixed[:, rows:], inv)
    gated = query_t[...] * (convolved + skip_col[...] * signal_t[...])
    out[...] = gated.T.astype(BF16)


def unpack_kernel(place, mine, other, grad_one, bias_one, grad_two, bias_two, grad_three, whole):
    half = mine.shape[0]
    bit = place[1]
    whole[pl.ds(pl.multiple_of(bit * half, 8), half), :] = mine[...]
    whole[pl.ds(pl.multiple_of((1 - bit) * half, 8), half), :] = other[...]
    order = grad_three.shape[0]
    slabs = grad_three.shape[1] // LANES
    for slab in range(slabs):
        grad_three[:, slab * LANES : (slab + 1) * LANES] = whole[
            slab * order : (slab + 1) * order, :
        ]
    at = slabs * order
    features = grad_one.shape[0]
    grad_one[...] = whole[at : at + features, :]
    grad_two[...] = whole[at + features : at + features + order, :]
    at = at + features + order
    bias_one[...] = whole[at : at + 1, :]
    bias_two[...] = whole[at + 8 : at + 9, :]


def run(kernel, ins, outs, scratch=(), flops=0, smem=()):
    in_specs = [
        pl.BlockSpec(memory_space=pltpu.SMEM if i in smem else pltpu.VMEM) for i in range(len(ins))
    ]
    moved = sum(math.prod(a.shape) * a.dtype.itemsize for a in list(ins) + list(outs))
    return pl.pallas_call(
        kernel,
        out_shape=tuple(outs),
        in_specs=in_specs,
        out_specs=tuple(pl.BlockSpec(memory_space=pltpu.VMEM) for _ in outs),
        scratch_shapes=list(scratch),
        compiler_params=pltpu.CompilerParams(vmem_limit_bytes=VMEM),
        cost_estimate=pl.CostEstimate(flops=flops, bytes_accessed=moved, transcendentals=0),
    )(*ins)


def swap_with(block, axis, distance):
    size = lax.axis_size(axis)
    return lax.ppermute(block, axis, [(i, i ^ distance) for i in range(size)])


def all_added(block):
    steps = [("dp", 1 << i) for i in range(1, lax.axis_size("dp").bit_length() - 1)]
    steps += [("seq", 1 << i) for i in range(lax.axis_size("seq").bit_length() - 1)]
    cut = (block.shape[0] // 2 + 7) // 8 * 8
    parts = [block[:cut], block[cut:]]
    turn = len(steps) // 2
    for s in range(len(steps)):
        moves = (steps[s], steps[(s + turn) % len(steps)])
        parts = [part + swap_with(part, *move) for part, move in zip(parts, moves)]
    return jnp.concatenate(parts, axis=0)


def body(tokens, embed, taps, skip, rates, w_one, b_one, w_two, b_two, w_three, cotangent):
    blocks = lax.axis_size("seq")
    own = lax.axis_index("seq")
    bit = lax.axis_index("dp") % 2
    rows = tokens.shape[1]
    channels = skip.shape[0]
    features, order = w_one.shape
    length = rows * blocks
    apart = blocks > CHUNK
    shape = jax.ShapeDtypeStruct
    place = jnp.stack([own, bit]).astype(jnp.int32)

    gathered = lax.all_to_all(
        jnp.broadcast_to(tokens, (blocks, rows)), "seq", split_axis=0, concat_axis=0, tiled=True
    )

    feat_high, feat_low = (jnp.asarray(t) for t in feature_tables(length, features // 2))
    first, inv, sign = (jnp.asarray(t) for t in transform_tables(rows))
    code, pick = (jnp.asarray(t) for t in letter_tables(LANES))
    wide = (order, length)
    bias_rows = (b_one.reshape(1, order), b_two.reshape(1, order))
    pre_ins = [
        embed[:LANES], taps, pick, rates.reshape(1, channels), skip.reshape(1, channels),
        cotangent[0], w_one, bias_rows[0], w_two, bias_rows[1], w_three,
    ]
    pre_outs = [shape((3 * channels, LANES), BF16)] + [shape((channels, LANES), F32)] * 3
    if not apart:
        pre_ins += [feat_high, feat_low, first]
        pre_outs += [shape(wide, BF16), shape(wide, BF16), shape(wide, F32)] * 2
        pre_outs += [shape((blocks, channels, 2 * rows), F32)]
    table, rates_col, skip_col, cot_t, *made = run(
        functools.partial(pre_kernel, length, apart), pre_ins, pre_outs, flops=2 * 10**9
    )

    total = channels // LANES * order + features + order + 16
    half = (total // 2 + 7) // 8 * 8
    count = min(blocks, CHUNK)
    slots = count if blocks == count else count + 1
    main_ins = [place, gathered, code, first, inv, sign, table, rates_col, cot_t]
    main_ins += [w_two, w_three, feat_high, feat_low]
    main_ins += [w_one, *bias_rows] if apart else made
    keep, send, mixed, query_t, signal_t = run(
        functools.partial(main_kernel, length, apart),
        main_ins,
        [shape((half, LANES), F32)] * 2
        + [shape((channels, 2 * rows), F32)]
        + [shape((channels, rows), F32)] * 2,
        scratch=[
            pltpu.VMEM((LANES, slots * rows), BF16),
            pltpu.VMEM((slots, channels, 2 * rows), F32),
            pltpu.VMEM((channels, count * rows), BF16),
            pltpu.VMEM((channels, count * rows), BF16),
            pltpu.VMEM((2 * half, LANES), F32),
        ],
        flops=6 * 10**9,
        smem=(0,),
    )
    summed = all_added(keep + swap_with(send, "dp", 1))
    (gated,) = run(
        gate_kernel,
        [mixed, inv, query_t, signal_t, skip_col],
        [shape((rows, channels), BF16)],
        flops=3 * 10**8,
    )
    other = swap_with(summed, "dp", 1)
    grad_one, bias_one, grad_two, bias_two, grad_three = run(
        unpack_kernel,
        [place, summed, other],
        [
            shape((features, order), F32), shape((1, order), F32), shape((order, order), F32),
            shape((1, order), F32), shape((order, channels), F32),
        ],
        scratch=[pltpu.VMEM((2 * half, LANES), F32)],
        smem=(0,),
    )
    return (
        gated[None], grad_one, bias_one.reshape(order), grad_two, bias_two.reshape(order),
        grad_three,
    )


def solution(mesh):
    return jax.shard_map(
        body,
        mesh=mesh,
        in_specs=(
            P("dp", "seq"),
            P(),
            P(),
            P(),
            P(),
            P(),
            P(),
            P(),
            P(),
            P(),
            P("dp", "seq", None),
        ),
        out_specs=(P("dp", "seq", None), P(), P(), P(), P(), P()),
        check_vma=False,
    )
```

```python
import functools
import math

import jax
import jax.numpy as jnp
import ml_dtypes
import numpy as np
from jax import lax
from jax.experimental import pallas as pl
from jax.experimental.pallas import tpu as pltpu
from jax.sharding import PartitionSpec as P

LETTERS = (65, 67, 71, 84, 97, 99, 103, 116, 78, 110)
GROUP = 16
LANES = 128
CHUNK = 8
SMALL = 24 * 1024 * 1024
LARGE = 56 * 1024 * 1024
F32 = jnp.float32
BF16 = jnp.bfloat16


def halves(table):
    high = table.astype(np.float32).astype(ml_dtypes.bfloat16)
    low = (table - high.astype(np.float64)).astype(np.float32).astype(ml_dtypes.bfloat16)
    return high, low


def band_numbers(length, band_count):
    return [
        max(band + 1, int(0.4 * length ** (band / (band_count - 1)))) for band in range(band_count)
    ]


@functools.cache
def feature_tables(length, band_count):
    numbers = np.array(band_numbers(length, band_count), np.int64)
    residue = (numbers[:, None] * np.arange(length, dtype=np.int64)[None, :]) % length
    angles = residue * (2.0 * math.pi / length)
    return np.concatenate(halves(np.concatenate([np.sin(angles), np.cos(angles)], axis=0)), axis=0)


@functools.cache
def transform_tables(rows):
    theta = np.pi * (np.arange(rows) + 0.5) / rows
    angles = np.arange(rows)[:, None] * theta[None, :]
    forward = np.concatenate([np.cos(angles), -np.sin(angles)], axis=1)
    high, low = halves(forward)
    first = np.concatenate([high, low], axis=0)
    inv_high, inv_low = halves(forward.T / rows)
    inverse = np.concatenate([inv_high, inv_low], axis=1)
    sign = np.broadcast_to(np.where(np.arange(rows) % 2 == 0, 1.0, -1.0), (8, rows))
    return first, inverse, sign.astype(np.float32)


@functools.cache
def letter_tables(lanes):
    code = np.full((lanes,), -1, np.int32)
    pick = np.zeros((lanes, lanes), np.float32)
    for row in range(6 * GROUP):
        if row % GROUP < len(LETTERS):
            code[row] = LETTERS[row % GROUP]
            pick[row, code[row]] = 1.0
    code = np.ascontiguousarray(np.broadcast_to(code[:, None], (lanes, lanes)))
    return code, pick.astype(ml_dtypes.bfloat16)


def split(x):
    high = x.astype(BF16)
    return high, (x - high.astype(F32)).astype(BF16)


def mm(a, b, ca=1, cb=0):
    return lax.dot_general(a, b, (((ca,), (cb,)), ((), ())), preferred_element_type=F32)


def left_mm(stack, high, low, cb=0):
    m = stack.shape[0] // 2
    both = mm(stack, high, cb=cb)
    return both[:m] + both[m:] + mm(stack[:m], low, cb=cb)


def sin_cos(x):
    turns = jnp.floor(x * (2.0 / math.pi) + 0.5)
    r = x - turns * 1.5703125
    r = r - turns * 4.837512969970703125e-4
    r = r - turns * 7.549789948768648e-8
    quarter = turns.astype(jnp.int32)
    z = r * r
    s = r + r * z * (-1.6666654611e-1 + z * (8.3321608736e-3 + z * -1.9515295891e-4))
    c = 1.0 + z * (
        -0.5 + z * (4.166664568298827e-2 + z * (-1.388731625493765e-3 + z * 2.443315711809948e-5))
    )
    swap = (quarter & 1) == 1
    sine = jnp.where(swap, c, s)
    cosine = jnp.where(swap, s, c)
    sine = jnp.where((quarter & 2) == 2, -sine, sine)
    cosine = jnp.where(((quarter + 1) & 2) == 2, -cosine, cosine)
    return sine, cosine


def forward(block, first_ref):
    rows = block.shape[1]
    high, low = split(block)
    return mm(jnp.concatenate([high, high], axis=1), first_ref[...]) + mm(low, first_ref[:rows, :])


def inverse(real, imag, inverse_ref):
    rows = real.shape[1]
    high, low = split(jnp.concatenate([real, imag], axis=1))
    both = mm(high, inverse_ref[...])
    return both[:, :rows] + both[:, rows:] + mm(low, inverse_ref[:, :rows])


def window_block(rates, start, rows, length):
    place = (lax.broadcasted_iota(jnp.int32, (1, rows), 1) + start).astype(F32) * (-1.0 / length)
    return jnp.exp(rates * place) * (1.0 / math.sqrt(length))


def prepare(w_one, w_two, w_three, b_one, b_two, order):
    one = jnp.concatenate(split(w_one.T), axis=0)
    two = jnp.concatenate(split(w_two.T), axis=0)
    three = jnp.concatenate(split(w_three.T), axis=0)
    col_one = jnp.broadcast_to(b_one, (order, order)).T
    col_two = jnp.broadcast_to(b_two, (order, order)).T
    return one, two, three, col_one, col_two


def network(feat, one, two, col_one, col_two):
    count = feat.shape[1] // LANES
    size = feat.shape[0] // 2
    act_one, cos_one = sin_cos(
        left_mm(one, feat[:size], feat[size:]) + jnp.concatenate([col_one] * count, axis=1)
    )
    one_high, one_low = split(act_one)
    act_two, cos_two = sin_cos(
        left_mm(two, one_high, one_low) + jnp.concatenate([col_two] * count, axis=1)
    )
    act_one = jnp.concatenate([one_high, one_low], axis=0)
    return act_one, cos_one, jnp.concatenate(split(act_two), axis=0), cos_two


def lookup_table(embed, taps, pick):
    chosen = mm(pick, embed)
    channels = taps.shape[2]
    pieces = []
    for branch in range(3):
        part = chosen[:, branch * channels : (branch + 1) * channels]
        scaled = [
            part[tap * GROUP : (tap + 1) * GROUP] * taps[branch, tap : tap + 1, :]
            for tap in range(3)
        ]
        high = jnp.concatenate(scaled, axis=0)
        rounded = high.astype(BF16).astype(F32)
        rest = jnp.zeros((LANES - 6 * GROUP, channels), F32)
        pieces.append(jnp.concatenate([rounded, high - rounded, rest], axis=0).T)
    return jnp.concatenate(pieces, axis=0).astype(BF16)


def one_hot(tok_ref, own, block, code):
    rows = tok_ref.shape[1]

    def row(j):
        got = tok_ref[pl.ds(jnp.maximum(j, 0) ^ own, 1), :]
        return jnp.where(j >= 0, got, 0)

    now = jnp.broadcast_to(row(block), (8, rows))
    before = jnp.broadcast_to(row(block - 1), (8, rows))
    lane = lax.broadcasted_iota(jnp.int32, (8, rows), 1)
    shifted = [now]
    for tap in (1, 2):
        shifted.append(
            jnp.where(lane < tap, pltpu.roll(before, tap, 1), pltpu.roll(now, tap, 1))
        )
    wide = [jnp.concatenate([s, s], axis=0) for s in shifted]
    rest = jnp.zeros((LANES - 6 * GROUP, rows), jnp.int32)
    spread = jnp.concatenate(wide + wide + [rest], axis=0)
    return jnp.where(spread == code, 1.0, 0.0).astype(BF16)


def network_kernel(apart, w_one, b_one, w_two, b_two, w_three, feat, *outs):
    two_back, three_back = outs[:2]
    two_back[...] = jnp.concatenate(split(w_two[...]), axis=0)
    three_back[...] = jnp.concatenate(split(w_three[...]), axis=0)
    order = w_one.shape[1]
    made = prepare(w_one[...], w_two[...], w_three[...], b_one[...], b_two[...], order)
    if not apart:
        one, two, three, col_one, col_two = made
        made = (*network(feat[...], one, two, col_one, col_two), three)
    for ref, value in zip(outs[2:], made):
        ref[...] = value


def filter_kernel(length, rates, act_two, three, first, rates_col, spectra):
    channels = rates.shape[1]
    order = act_two.shape[0] // 2
    rates_col[...] = jnp.broadcast_to(rates[...], (LANES, channels)).T
    for k in range(length // LANES):
        at = slice(k * LANES, (k + 1) * LANES)
        filt = left_mm(three[...], act_two[:order, at], act_two[order:, at])
        filt = filt * window_block(rates_col[...], k * LANES, LANES, length)
        spectra[k] = forward(filt, first)


def table_kernel(embed_all, taps, pick, skip, rates, cot, table, skip_col, rates_col, cot_t, embed):
    pltpu.sync_copy(embed_all.at[pl.ds(0, LANES), :], embed)
    channels = cot.shape[1]
    table[...] = lookup_table(embed[...], taps[...], pick[...])
    skip_col[...] = jnp.broadcast_to(skip[...], (LANES, channels)).T
    rates_col[...] = jnp.broadcast_to(rates[...], (LANES, channels)).T
    cot_t[...] = cot[...].astype(F32).T


def main_kernel(length, apart, *refs):
    tok = refs[0]
    table, rates_col, cot_t, feat, first, inv, sign, code, two_back, three_back = refs[1:11]
    if apart:
        one_t, two_t, three_t, col_one, col_two = (r[...] for r in refs[11:16])
    else:
        one_all, cos_one, two_all, cos_two, spectra = refs[11:16]
    keep, send, mixed, query_t, signal_t = refs[16:21]
    hot, spec, slope_high, slope_low, packed = refs[21:26]
    blocks, rows = tok.shape
    channels = cot_t.shape[0]
    order = two_back.shape[1]
    count = min(blocks, CHUNK)
    chunks = blocks // count
    own = lax.axis_index("seq")
    bit = lax.axis_index("dp") % 2
    codes = code[...]
    signs = jnp.broadcast_to(sign[0:1, :], (channels, rows))

    own_hot = one_hot(tok, own, own, codes)
    query = mm(table[:channels, :], own_hot)
    query_t[...] = query
    up = forward(cot_t[...] * query, first)
    up_real, up_imag = up[:, :rows], up[:, rows:]

    def chunk(base):
        static = isinstance(base, int)
        slots = count if static else count + 1
        lane0 = base * rows if static else pl.multiple_of(base * rows, rows * count)
        for i in range(slots):
            hot[:, i * rows : (i + 1) * rows] = one_hot(tok, own, own - base - i, codes)
        span = pl.ds(lane0, count * rows)
        if apart:
            act_one, cosine_one, act_two, cosine_two = network(
                feat[:, span], one_t, two_t, col_one, col_two
            )
        else:
            act_one, cosine_one, act_two, cosine_two = (
                r[:, span] for r in (one_all, cos_one, two_all, cos_two)
            )
        for i in range(slots):
            both = mm(table[channels:, :], hot[:, i * rows : (i + 1) * rows])
            signal = both[:channels] * both[channels:]
            if i == 0:
                if static:
                    signal_t[...] = signal
                else:

                    @pl.when(base == 0)
                    def _():
                        signal_t[...] = signal

            spec[i] = forward(signal, first)
        for i in range(count):
            real, imag = spec[i, :, :rows], spec[i, :, rows:]
            if i + 1 < slots:
                real = real - signs * spec[i + 1, :, rows:]
                imag = imag + signs * spec[i + 1, :, :rows]
            weight = window_block(rates_col[...], lane0 + i * rows, rows, length)
            if apart:
                at = slice(i * rows, (i + 1) * rows)
                filt = left_mm(three_t, act_two[:order, at], act_two[order:, at]) * weight
                got = forward(filt, first)
            else:
                got = spectra[base + i]
            g_real, g_imag = got[:, :rows], got[:, rows:]
            add_real = g_real * real - g_imag * imag
            add_imag = g_real * imag + g_imag * real
            if static and i == 0:
                mixed[:, :rows] = add_real
                mixed[:, rows:] = add_imag
            else:
                mixed[:, :rows] += add_real
                mixed[:, rows:] += add_imag
            lag = inverse(
                up_real * real + up_imag * imag, up_imag * real - up_real * imag, inv
            )
            high, low = split(lag * weight)
            slope_high[:, i * rows : (i + 1) * rows] = high
            slope_low[:, i * rows : (i + 1) * rows] = low

        def put(at, value):
            if static:
                packed[at : at + value.shape[0], :] = value
            else:
                packed[at : at + value.shape[0], :] += value

        slopes_high, slopes_low = slope_high[...], slope_low[...]
        grad_three = left_mm(act_two, slopes_high, slopes_low, cb=1)
        for slab in range(channels // LANES):
            put(slab * order, grad_three[:, slab * LANES : (slab + 1) * LANES])
        back_two = left_mm(three_back[...], slopes_high, slopes_low) * cosine_two
        two_split = split(back_two)
        back_one = left_mm(two_back[...], *two_split) * cosine_one
        one_split = split(back_one)
        grad_two = left_mm(act_one, *two_split, cb=1)
        grad_one = left_mm(feat[:, span], *one_split, cb=1)
        ones = jnp.ones((8, count * rows), BF16)
        at = channels // LANES * order
        put(at, grad_one)
        at = at + grad_one.shape[0]
        put(at, grad_two)
        at = at + order
        put(at, mm(ones, one_split[0], cb=1) + mm(ones, one_split[1], cb=1))
        put(at + 8, mm(ones, two_split[0], cb=1) + mm(ones, two_split[1], cb=1))
        at = at + 16
        if static and packed.shape[0] > at:
            packed[at:, :] = jnp.zeros((packed.shape[0] - at, LANES), F32)

    if chunks == 1:
        chunk(0)
    else:
        mixed[...] = jnp.zeros(mixed.shape, F32)
        packed[...] = jnp.zeros(packed.shape, F32)

        @pl.loop(0, chunks)
        def _(q):
            chunk(q * count)

    half = keep.shape[0]
    keep[...] = packed[pl.ds(pl.multiple_of(bit * half, 8), half), :]
    send[...] = packed[pl.ds(pl.multiple_of((1 - bit) * half, 8), half), :]


def gate_kernel(mixed, inv, query_t, signal_t, skip_col, out):
    rows = query_t.shape[1]
    convolved = inverse(mixed[:, :rows], mixed[:, rows:], inv)
    gated = query_t[...] * (convolved + skip_col[...] * signal_t[...])
    out[...] = gated.T.astype(BF16)


def unpack_kernel(mine, other, grad_one, bias_one, grad_two, bias_two, grad_three, whole):
    half = mine.shape[0]
    bit = lax.axis_index("dp") % 2
    whole[pl.ds(pl.multiple_of(bit * half, 8), half), :] = mine[...]
    whole[pl.ds(pl.multiple_of((1 - bit) * half, 8), half), :] = other[...]
    order = grad_three.shape[0]
    slabs = grad_three.shape[1] // LANES
    for slab in range(slabs):
        grad_three[:, slab * LANES : (slab + 1) * LANES] = whole[
            slab * order : (slab + 1) * order, :
        ]
    at = slabs * order
    features = grad_one.shape[0]
    grad_one[...] = whole[at : at + features, :]
    grad_two[...] = whole[at + features : at + features + order, :]
    at = at + features + order
    bias_one[...] = whole[at : at + 1, :]
    bias_two[...] = whole[at + 8 : at + 9, :]


def run(kernel, ins, outs, scratch=(), flops=0, far=(), limit=SMALL):
    moved = sum(math.prod(a.shape) * a.dtype.itemsize for a in list(ins) + list(outs))
    return pl.pallas_call(
        kernel,
        out_shape=tuple(outs),
        in_specs=[
            pl.BlockSpec(memory_space=pl.ANY if i in far else pltpu.VMEM) for i in range(len(ins))
        ],
        out_specs=tuple(pl.BlockSpec(memory_space=pltpu.VMEM) for _ in outs),
        scratch_shapes=list(scratch),
        compiler_params=pltpu.CompilerParams(vmem_limit_bytes=limit),
        cost_estimate=pl.CostEstimate(flops=flops, bytes_accessed=moved, transcendentals=0),
    )(*ins)


def swap_with(block, axis, distance):
    size = lax.axis_size(axis)
    return lax.ppermute(block, axis, [(i, i ^ distance) for i in range(size)])


def all_rows(row):
    rows = row
    for step in range(lax.axis_size("seq").bit_length() - 1):
        rows = jnp.concatenate([rows, swap_with(rows, "seq", 1 << step)], axis=0)
    return rows


def all_added(block, beside):
    steps = [("dp", 1 << i) for i in range(1, lax.axis_size("dp").bit_length() - 1)]
    steps += [("seq", 1 << i) for i in range(lax.axis_size("seq").bit_length() - 1)]
    cut = (block.shape[0] // 2 + 7) // 8 * 8
    parts = [block[:cut], block[cut:]]
    turn = len(steps) // 2
    for s in range(len(steps)):
        moves = (steps[s], steps[(s + turn) % len(steps)])
        parts = [part + swap_with(part, *move) for part, move in zip(parts, moves)]
        if s == 1:
            parts[0], beside = lax.optimization_barrier((parts[0], beside))
    return jnp.concatenate(parts, axis=0), beside


def body(tokens, embed, taps, skip, rates, w_one, b_one, w_two, b_two, w_three, cotangent):
    blocks = lax.axis_size("seq")
    rows = tokens.shape[1]
    channels = skip.shape[0]
    features, order = w_one.shape
    length = rows * blocks
    apart = blocks > CHUNK
    limit = LARGE if apart else SMALL
    shape = jax.ShapeDtypeStruct

    gathered = all_rows(tokens)

    feat = jnp.asarray(feature_tables(length, features // 2))
    first, inv, sign = (jnp.asarray(t) for t in transform_tables(rows))
    code, pick = (jnp.asarray(t) for t in letter_tables(LANES))
    rates_row = rates.reshape(1, channels)
    wide = (order, length)
    net_outs = [shape((2 * order, order), BF16), shape((2 * order, channels), BF16)]
    if apart:
        net_outs += [shape((2 * order, features), BF16), shape((2 * order, order), BF16)]
        net_outs += [shape((2 * channels, order), BF16)] + [shape((order, LANES), F32)] * 2
    else:
        net_outs += [shape((2 * order, length), BF16), shape(wide, F32)] * 2
        net_outs += [shape((2 * channels, order), BF16)]
    two_back, three_back, *made = run(
        functools.partial(network_kernel, apart),
        [w_one, b_one.reshape(1, order), w_two, b_two.reshape(1, order), w_three, feat],
        net_outs,
        flops=10**9,
        limit=limit,
    )
    column = shape((channels, LANES), F32)
    table, skip_col, rates_col, cot_t = run(
        table_kernel,
        [embed, taps, pick, skip.reshape(1, channels), rates_row, cotangent[0]],
        [shape((3 * channels, LANES), BF16), column, column, column],
        scratch=[pltpu.VMEM((LANES, embed.shape[1]), embed.dtype)],
        flops=10**9,
        far=(0,),
        limit=limit,
    )
    if not apart:
        rates_col, spectra = run(
            functools.partial(filter_kernel, length),
            [rates_row, made[2], made[4], first],
            [column, shape((blocks, channels, 2 * rows), F32)],
            flops=2 * 10**9,
            limit=limit,
        )
        made[4] = spectra

    total = channels // LANES * order + features + order + 16
    half = (total // 2 + 7) // 8 * 8
    count = min(blocks, CHUNK)
    slots = count if blocks == count else count + 1
    keep, send, mixed, query_t, signal_t = run(
        functools.partial(main_kernel, length, apart),
        [gathered, table, rates_col, cot_t, feat, first, inv, sign, code, two_back, three_back]
        + made,
        [shape((half, LANES), F32)] * 2
        + [shape((channels, 2 * rows), F32)]
        + [shape((channels, rows), F32)] * 2,
        scratch=[
            pltpu.VMEM((LANES, slots * rows), BF16),
            pltpu.VMEM((slots, channels, 2 * rows), F32),
            pltpu.VMEM((channels, count * rows), BF16),
            pltpu.VMEM((channels, count * rows), BF16),
            pltpu.VMEM((2 * half, LANES), F32),
        ],
        flops=6 * 10**9,
        limit=limit,
    )
    (gated,) = run(
        gate_kernel,
        [mixed, inv, query_t, signal_t, skip_col],
        [shape((rows, channels), BF16)],
        flops=3 * 10**8,
        limit=limit,
    )
    summed, gated = all_added(keep + swap_with(send, "dp", 1), gated)
    other = swap_with(summed, "dp", 1)
    grad_one, bias_one, grad_two, bias_two, grad_three = run(
        unpack_kernel,
        [summed, other],
        [
            shape((features, order), F32), shape((1, order), F32), shape((order, order), F32),
            shape((1, order), F32), shape((order, channels), F32),
        ],
        scratch=[pltpu.VMEM((2 * half, LANES), F32)],
    )
    return (
        gated[None], grad_one, bias_one.reshape(order), grad_two, bias_two.reshape(order),
        grad_three,
    )


def solution(mesh):
    return jax.shard_map(
        body,
        mesh=mesh,
        in_specs=(
            P("dp", "seq"),
            P(),
            P(),
            P(),
            P(),
            P(),
            P(),
            P(),
            P(),
            P(),
            P("dp", "seq", None),
        ),
        out_specs=(P("dp", "seq", None), P(), P(), P(), P(), P()),
        check_vma=False,
    )
```

```python
import functools
import math

import jax
import jax.numpy as jnp
import ml_dtypes
import numpy as np
from jax import lax
from jax.experimental import pallas as pl
from jax.experimental.pallas import tpu as pltpu
from jax.sharding import PartitionSpec as P

LETTERS = (65, 67, 71, 84, 97, 99, 103, 116, 78, 110)
GROUP = 16
LANES = 128
CHUNK = 8
SMALL = 24 * 1024 * 1024
LARGE = 56 * 1024 * 1024
F32 = jnp.float32
BF16 = jnp.bfloat16


def halves(table):
    high = table.astype(np.float32).astype(ml_dtypes.bfloat16)
    low = (table - high.astype(np.float64)).astype(np.float32).astype(ml_dtypes.bfloat16)
    return high, low


def band_numbers(length, band_count):
    return [
        max(band + 1, int(0.4 * length ** (band / (band_count - 1)))) for band in range(band_count)
    ]


@functools.cache
def feature_tables(length, band_count):
    numbers = np.array(band_numbers(length, band_count), np.int64)
    residue = (numbers[:, None] * np.arange(length, dtype=np.int64)[None, :]) % length
    angles = residue * (2.0 * math.pi / length)
    return np.concatenate(halves(np.concatenate([np.sin(angles), np.cos(angles)], axis=0)), axis=0)


@functools.cache
def transform_tables(rows):
    theta = np.pi * (np.arange(rows) + 0.5) / rows
    angles = np.arange(rows)[:, None] * theta[None, :]
    forward = np.concatenate([np.cos(angles), -np.sin(angles)], axis=1)
    high, low = halves(forward)
    first = np.concatenate([high, low, high], axis=0)
    inv_high, inv_low = halves(forward.T / rows)
    inverse = np.concatenate([inv_high, inv_low], axis=1)
    sign = np.broadcast_to(np.where(np.arange(rows) % 2 == 0, 1.0, -1.0), (8, rows))
    return first, inverse, sign.astype(np.float32)


@functools.cache
def letter_tables(lanes):
    code = np.full((lanes,), -1, np.int32)
    pick = np.zeros((lanes, lanes), np.float32)
    for row in range(6 * GROUP):
        if row % GROUP < len(LETTERS):
            code[row] = LETTERS[row % GROUP]
            pick[row, code[row]] = 1.0
    code = np.ascontiguousarray(np.broadcast_to(code[:, None], (lanes, lanes)))
    return code, pick.astype(ml_dtypes.bfloat16)


def split(x):
    high = x.astype(BF16)
    return high, (x - high.astype(F32)).astype(BF16)


def mm(a, b, ca=1, cb=0):
    return lax.dot_general(a, b, (((ca,), (cb,)), ((), ())), preferred_element_type=F32)


def left_mm(stack, high, low, cb=0):
    m = stack.shape[0] // 2
    both = mm(stack, high, cb=cb)
    return both[:m] + both[m:] + mm(stack[:m], low, cb=cb)


def sin_cos(x):
    turns = jnp.floor(x * (1.0 / math.pi) + 0.5)
    r = x - turns * 3.140625
    r = r - turns * 9.67653589793116e-4
    z = r * r
    s = -0.0001980613308286788 + z * 2.599125898339353e-06
    s = -0.16666656691981288 + z * (0.00833300936890471 + z * s)
    c = 2.476157712136818e-05 + z * -2.607203341358802e-07
    c = -0.49999999533050865 + z * (0.04166664015321537 + z * (-0.0013888396896628193 + z * c))
    half = turns * 0.5
    sign = 1.0 - 4.0 * (half - jnp.floor(half))
    return sign * (r + r * z * s), sign + (sign * z) * c


def forward(block, first_ref):
    high, low = split(block)
    return mm(jnp.concatenate([high, high, low], axis=1), first_ref[...])


def inverse(real, imag, inverse_ref):
    rows = real.shape[1]
    high, low = split(jnp.concatenate([real, imag], axis=1))
    both = mm(high, inverse_ref[...])
    return both[:, :rows] + both[:, rows:] + mm(low, inverse_ref[:, :rows])


def window_block(rates, start, rows, length):
    place = (lax.broadcasted_iota(jnp.int32, (1, rows), 1) + start).astype(F32) * (-1.0 / length)
    return jnp.exp(rates * place) * (1.0 / math.sqrt(length))


def window_step(rates, rows, length):
    return jnp.exp(rates * (-rows / length))


def column_stack(weights):
    return jnp.concatenate(split(weights.T), axis=0)


def row_stack(weights):
    high, low = split(weights.T)
    return jnp.concatenate([high, high, low], axis=1)


def layer(stack, values, bias):
    size = values.shape[0] // 2
    count = values.shape[1] // LANES
    column = jnp.broadcast_to(bias, (LANES, bias.shape[1])).T
    sine, cosine = sin_cos(
        left_mm(stack, values[:size], values[size:]) + jnp.concatenate([column] * count, axis=1)
    )
    return jnp.concatenate(split(sine), axis=0), cosine


def lookup_table(embed, taps, pick):
    chosen = mm(pick, embed)
    channels = taps.shape[2]
    pieces = []
    for branch in range(3):
        part = chosen[:, branch * channels : (branch + 1) * channels]
        scaled = [
            part[tap * GROUP : (tap + 1) * GROUP] * taps[branch, tap : tap + 1, :]
            for tap in range(3)
        ]
        high = jnp.concatenate(scaled, axis=0)
        rounded = high.astype(BF16).astype(F32)
        rest = jnp.zeros((LANES - 6 * GROUP, channels), F32)
        pieces.append(jnp.concatenate([rounded, high - rounded, rest], axis=0).T)
    return jnp.concatenate(pieces, axis=0).astype(BF16)


def one_hot(tok_ref, own, block, code):
    rows = tok_ref.shape[1]

    def row(j):
        got = tok_ref[pl.ds(jnp.maximum(j, 0) ^ own, 1), :]
        return jnp.where(j >= 0, got, 0)

    now = jnp.broadcast_to(row(block), (8, rows))
    before = jnp.broadcast_to(row(block - 1), (8, rows))
    lane = lax.broadcasted_iota(jnp.int32, (8, rows), 1)
    shifted = [now]
    for tap in (1, 2):
        shifted.append(
            jnp.where(lane < tap, pltpu.roll(before, tap, 1), pltpu.roll(now, tap, 1))
        )
    wide = [jnp.concatenate([s, s], axis=0) for s in shifted]
    rest = jnp.zeros((LANES - 6 * GROUP, rows), jnp.int32)
    spread = jnp.concatenate(wide + wide + [rest], axis=0)
    return jnp.where(spread == code, 1.0, 0.0).astype(BF16)


def fetch(sources, targets, sems):
    copies = []
    for m, (source, target) in enumerate(zip(sources, targets)):
        if source.shape != target.shape:
            source = source.at[pl.ds(0, target.shape[0]), :]
        copies.append(pltpu.make_async_copy(source, target, sems.at[m]))
    for copy in copies:
        copy.start()
    return copies


def first_kernel(w_one, b_one, feat, act_one, cos_one):
    act, cosine = layer(column_stack(w_one[...]), feat[...], b_one[...])
    act_one[...] = act
    cos_one[...] = cosine


def second_kernel(apart, w_two, b_two, w_three, *refs):
    two_back, three_back = refs[-4:-2] if not apart else refs
    two_back[...] = jnp.concatenate(split(w_two[...]), axis=0)
    three_back[...] = jnp.concatenate(split(w_three[...]), axis=0)
    if not apart:
        act, cosine = layer(column_stack(w_two[...]), refs[0][...], b_two[...])
        refs[-2][...] = act
        refs[-1][...] = cosine


def table_kernel(count, *refs):
    sources, targets = refs[:count], refs[count : 2 * count - 6]
    table, skip_col, rates_col, cot_t = refs[2 * count - 6 : 2 * count - 2]
    embed, taps, pick, skip, rates, cot = refs[2 * count - 2 : -1]
    copies = fetch(sources, (embed, taps, pick, skip, rates, cot, *targets), refs[-1])
    for copy in copies[:6]:
        copy.wait()
    channels = cot.shape[1]
    table[...] = lookup_table(embed[...], taps[...], pick[...])
    skip_col[...] = jnp.broadcast_to(skip[...], (LANES, channels)).T
    rates_col[...] = jnp.broadcast_to(rates[...], (LANES, channels)).T
    cot_t[...] = cot[...].astype(F32).T
    for copy in copies[6:]:
        copy.wait()


def filter_kernel(length, rates_col, act_two, w_three, first, spectra, window, step):
    order = act_two.shape[0] // 2
    three = row_stack(w_three[...])
    window[...] = window_block(rates_col[...], 0, LANES, length)
    step[...] = window_step(rates_col[...], LANES, length)
    for k in range(0, length // LANES, 2):
        pair = min(2, length // LANES - k)
        at = slice(k * LANES, (k + pair) * LANES)
        filt = mm(three, jnp.concatenate([act_two[:, at], act_two[:order, at]], axis=0))
        for m in range(pair):
            if k + m:
                window[...] *= step[...]
            spectra[k + m] = forward(filt[:, m * LANES : (m + 1) * LANES] * window[...], first)


def shifted_sum(spec, i, slots, signs):
    rows = signs.shape[1]
    real, imag = spec[i, :, :rows], spec[i, :, rows:]
    if i + 1 < slots:
        real = real - signs * spec[i + 1, :, rows:]
        imag = imag + signs * spec[i + 1, :, :rows]
    return real, imag


def main_kernel(length, apart, *refs):
    tok = refs[0]
    table, rates_col, cot_t, feat, first, inv, sign, code, two_back, three_back = refs[1:11]
    if apart:
        w_one, b_one, w_two, b_two, w_three = refs[11:16]
        one_t, two_t = column_stack(w_one[...]), column_stack(w_two[...])
        three_t = row_stack(w_three[...])
        keep, send, query_t, signal_t, mixed, spec = refs[16:22]
    else:
        one_all, cos_one, two_all, cos_two = refs[11:15]
        keep, send, query_t, signal_t, spec = refs[15:20]
    hot, slope_high, slope_low, packed, window, step = refs[-6:]
    blocks, rows = tok.shape
    channels = cot_t.shape[0]
    order = two_back.shape[1]
    count = min(blocks, CHUNK)
    chunks = blocks // count
    own = lax.axis_index("seq")
    bit = lax.axis_index("dp") % 2
    codes = code[...]
    signs = jnp.broadcast_to(sign[0:1, :], (channels, rows))

    step[...] = window_step(rates_col[...], rows, length)
    own_hot = one_hot(tok, own, own, codes)
    query = mm(table[:channels, :], own_hot)
    query_t[...] = query
    up = forward(cot_t[...] * query, first)
    up_real, up_imag = up[:, :rows], up[:, rows:]

    def chunk(base):
        static = isinstance(base, int)
        slots = count if static else count + 1
        lane0 = base * rows if static else pl.multiple_of(base * rows, rows * count)
        for i in range(slots):
            hot[:, i * rows : (i + 1) * rows] = one_hot(tok, own, own - base - i, codes)
        span = pl.ds(lane0, count * rows)
        if apart:
            act_one, cosine_one = layer(one_t, feat[:, span], b_one[...])
            act_two, cosine_two = layer(two_t, act_one, b_two[...])
        else:
            act_one, cosine_one, act_two, cosine_two = (
                r[:, span] for r in (one_all, cos_one, two_all, cos_two)
            )
        for i in range(0, slots, 2):
            pair = min(2, slots - i)
            both = mm(table[channels:, :], hot[:, i * rows : (i + pair) * rows])
            signals = both[:channels] * both[channels:]
            for m in range(pair):
                signal = signals[:, m * rows : (m + 1) * rows]
                if i + m == 0:
                    if static:
                        signal_t[...] = signal
                    else:

                        @pl.when(base == 0)
                        def _():
                            signal_t[...] = signal

                spec[i + m] = forward(signal, first)
        for i in range(count):
            real, imag = shifted_sum(spec, i, slots, signs)
            if i == 0:
                window[...] = window_block(rates_col[...], lane0, rows, length)
            else:
                window[...] *= step[...]
            weight = window[...]
            if apart:
                at = slice(i * rows, (i + 1) * rows)
                filt = mm(three_t, jnp.concatenate([act_two[:, at], act_two[:order, at]], axis=0))
                got = forward(filt * weight, first)
                g_real, g_imag = got[:, :rows], got[:, rows:]
                mixed[:, :rows] += g_real * real - g_imag * imag
                mixed[:, rows:] += g_real * imag + g_imag * real
            lag = inverse(
                up_real * real + up_imag * imag, up_imag * real - up_real * imag, inv
            )
            high, low = split(lag * weight)
            slope_high[:, i * rows : (i + 1) * rows] = high
            slope_low[:, i * rows : (i + 1) * rows] = low

        def put(at, value):
            if static:
                packed[at : at + value.shape[0], :] = value
            else:
                packed[at : at + value.shape[0], :] += value

        slopes_high, slopes_low = slope_high[...], slope_low[...]
        grad_three = left_mm(act_two, slopes_high, slopes_low, cb=1)
        for slab in range(channels // LANES):
            put(slab * order, grad_three[:, slab * LANES : (slab + 1) * LANES])
        back_two = left_mm(three_back[...], slopes_high, slopes_low) * cosine_two
        two_split = split(back_two)
        back_one = left_mm(two_back[...], *two_split) * cosine_one
        one_split = split(back_one)
        grad_two = left_mm(act_one, *two_split, cb=1)
        grad_one = left_mm(feat[:, span], *one_split, cb=1)
        ones = jnp.ones((8, count * rows), BF16)
        at = channels // LANES * order
        put(at, grad_one)
        at = at + grad_one.shape[0]
        put(at, grad_two)
        at = at + order
        put(at, mm(ones, one_split[0], cb=1) + mm(ones, one_split[1], cb=1))
        put(at + 8, mm(ones, two_split[0], cb=1) + mm(ones, two_split[1], cb=1))
        at = at + 16
        if static and packed.shape[0] > at:
            packed[at:, :] = jnp.zeros((packed.shape[0] - at, LANES), F32)

    if chunks == 1:
        chunk(0)
    else:
        if apart:
            mixed[...] = jnp.zeros(mixed.shape, F32)
        packed[...] = jnp.zeros(packed.shape, F32)

        @pl.loop(0, chunks)
        def _(q):
            chunk(q * count)

    half = keep.shape[0]
    keep[...] = packed[pl.ds(pl.multiple_of(bit * half, 8), half), :]
    send[...] = packed[pl.ds(pl.multiple_of((1 - bit) * half, 8), half), :]


def gate_kernel(apart, *refs):
    query_t, signal_t, skip_col, inv, sign, *mix, out = refs
    rows = query_t.shape[1]
    if apart:
        total = [mix[0][:, :rows], mix[0][:, rows:]]
    else:
        spec, spectra = mix
        signs = jnp.broadcast_to(sign[0:1, :], query_t.shape)
        total = [jnp.zeros(query_t.shape, F32)] * 2
        for i in range(spec.shape[0]):
            real, imag = shifted_sum(spec, i, spec.shape[0], signs)
            g_real, g_imag = spectra[i, :, :rows], spectra[i, :, rows:]
            total[0] += g_real * real - g_imag * imag
            total[1] += g_real * imag + g_imag * real
    convolved = inverse(*total, inv)
    gated = query_t[...] * (convolved + skip_col[...] * signal_t[...])
    out[...] = gated.T.astype(BF16)


def unpack_kernel(mine, other, grad_one, bias_one, grad_two, bias_two, grad_three, whole):
    half = mine.shape[0]
    bit = lax.axis_index("dp") % 2
    whole[pl.ds(pl.multiple_of(bit * half, 8), half), :] = mine[...]
    whole[pl.ds(pl.multiple_of((1 - bit) * half, 8), half), :] = other[...]
    order = grad_three.shape[0]
    slabs = grad_three.shape[1] // LANES
    for slab in range(slabs):
        grad_three[:, slab * LANES : (slab + 1) * LANES] = whole[
            slab * order : (slab + 1) * order, :
        ]
    at = slabs * order
    features = grad_one.shape[0]
    grad_one[...] = whole[at : at + features, :]
    grad_two[...] = whole[at + features : at + features + order, :]
    at = at + features + order
    bias_one[...] = whole[at : at + 1, :]
    bias_two[...] = whole[at + 8 : at + 9, :]


def run(kernel, ins, outs, scratch=(), flops=0, far=False, limit=SMALL):
    moved = sum(math.prod(a.shape) * a.dtype.itemsize for a in list(ins) + list(outs))
    if far:
        ins = [pltpu.with_memory_space_constraint(a, pltpu.HBM) for a in ins]
    return pl.pallas_call(
        kernel,
        out_shape=tuple(outs),
        in_specs=[pl.BlockSpec(memory_space=pl.ANY if far else pltpu.VMEM)] * len(ins),
        out_specs=tuple(pl.BlockSpec(memory_space=pltpu.VMEM) for _ in outs),
        scratch_shapes=list(scratch),
        compiler_params=pltpu.CompilerParams(vmem_limit_bytes=limit),
        cost_estimate=pl.CostEstimate(flops=flops, bytes_accessed=moved, transcendentals=0),
    )(*ins)


def swap_with(block, axis, distance):
    size = lax.axis_size(axis)
    return lax.ppermute(block, axis, [(i, i ^ distance) for i in range(size)])


def all_rows(row, same_row):
    rows = jnp.concatenate([same_row, swap_with(row, "seq", 1)], axis=0)
    for step in range(1, lax.axis_size("seq").bit_length() - 1):
        rows = jnp.concatenate([rows, swap_with(rows, "seq", 1 << step)], axis=0)
    return rows


def all_added(block, first_beside, second_beside):
    steps = [("dp", 1 << i) for i in range(1, lax.axis_size("dp").bit_length() - 1)]
    steps += [("seq", 1 << i) for i in range(lax.axis_size("seq").bit_length() - 1)]
    cut = (block.shape[0] // 2 + 7) // 8 * 8
    parts = [block[:cut], block[cut:]]
    made = first_beside(block)
    turn = len(steps) // 2
    for s in range(len(steps)):
        moves = (steps[s], steps[(s + turn) % len(steps)])
        parts = [part + swap_with(part, *move) for part, move in zip(parts, moves)]
        if s == 0:
            parts[1], made = lax.optimization_barrier((parts[1], made))
            made = second_beside(made)
        if s == 1:
            parts[0], made = lax.optimization_barrier((parts[0], made))
    return jnp.concatenate(parts, axis=0), made


def body(tokens, embed, taps, skip, rates, w_one, b_one, w_two, b_two, w_three, cotangent):
    blocks = lax.axis_size("seq")
    rows = tokens.shape[1]
    channels = skip.shape[0]
    features, order = w_one.shape
    length = rows * blocks
    apart = blocks > CHUNK
    limit = LARGE if apart else SMALL
    shape = jax.ShapeDtypeStruct

    feat = jnp.asarray(feature_tables(length, features // 2))
    first, inv, sign = (jnp.asarray(t) for t in transform_tables(rows))
    code, pick = (jnp.asarray(t) for t in letter_tables(LANES))
    wide = (order, length)
    column = shape((channels, LANES), F32)
    held = [
        embed, taps, pick, skip.reshape(1, channels), rates.reshape(1, channels), cotangent[0],
        w_one, b_one.reshape(1, order), feat, w_two, b_two.reshape(1, order), w_three, tokens,
        first, inv, sign, code,
    ]
    shapes = [shape(a.shape, a.dtype) for a in held]
    shapes[0] = shape((LANES, embed.shape[1]), embed.dtype)
    near = run(
        functools.partial(table_kernel, len(held)),
        held,
        shapes[6:] + [shape((3 * channels, LANES), BF16), column, column, column],
        scratch=[pltpu.VMEM(a.shape, a.dtype) for a in shapes[:6]]
        + [pltpu.SemaphoreType.DMA((len(held),))],
        flops=5 * 10**8,
        far=True,
        limit=limit,
    )
    w_one, b_one, feat, w_two, b_two, w_three, own_tokens, first, inv, sign, code = near[:11]
    table, skip_col, rates_col, cot_t = near[11:]
    gathered = all_rows(tokens, own_tokens)
    act_one = []
    layer_outs = [] if apart else [shape((2 * order, length), BF16), shape(wide, F32)]
    if not apart:
        act_one = run(
            first_kernel, [w_one, b_one, feat], layer_outs, flops=5 * 10**8, limit=limit
        )
    two_back, three_back, *act_two = run(
        functools.partial(second_kernel, apart),
        [w_two, b_two, w_three, *act_one[:1]],
        [shape((2 * order, order), BF16), shape((2 * order, channels), BF16)] + layer_outs,
        flops=5 * 10**8,
        limit=limit,
    )

    total = channels // LANES * order + features + order + 16
    half = (total // 2 + 7) // 8 * 8
    count = min(blocks, CHUNK)
    slots = count if blocks == count else count + 1
    spec_shape = (slots, channels, 2 * rows)
    main_outs = [shape((half, LANES), F32)] * 2 + [shape((channels, rows), F32)] * 2
    scratch = [
        pltpu.VMEM((LANES, slots * rows), BF16),
        pltpu.VMEM((channels, count * rows), BF16),
        pltpu.VMEM((channels, count * rows), BF16),
        pltpu.VMEM((2 * half, LANES), F32),
        pltpu.VMEM((channels, rows), F32),
        pltpu.VMEM((channels, rows), F32),
    ]
    if apart:
        main_outs += [shape((channels, 2 * rows), F32)]
        scratch = [pltpu.VMEM(spec_shape, F32)] + scratch
    else:
        main_outs += [shape(spec_shape, F32)]
    main_ins = [gathered, table, rates_col, cot_t, feat, first, inv, sign, code, two_back]
    keep, send, query_t, signal_t, mix = run(
        functools.partial(main_kernel, length, apart),
        main_ins
        + [three_back]
        + ([w_one, b_one, w_two, b_two, w_three] if apart else [*act_one, *act_two]),
        main_outs,
        scratch=scratch,
        flops=6 * 10**9,
        limit=limit,
    )

    def first_beside(held_back):
        if apart:
            return ()
        act, _ = lax.optimization_barrier((act_two[0], held_back))
        return run(
            functools.partial(filter_kernel, length),
            [rates_col, act, w_three, first],
            [shape((blocks, channels, 2 * rows), F32)],
            scratch=[pltpu.VMEM((channels, LANES), F32)] * 2,
            flops=2 * 10**9,
            limit=limit,
        )

    def second_beside(spectra):
        (gated,) = run(
            functools.partial(gate_kernel, apart),
            [query_t, signal_t, skip_col, inv, sign, mix, *spectra],
            [shape((rows, channels), BF16)],
            flops=10**9,
            limit=limit,
        )
        return gated

    summed, gated = all_added(keep + swap_with(send, "dp", 1), first_beside, second_beside)
    other = swap_with(summed, "dp", 1)
    grad_one, bias_one, grad_two, bias_two, grad_three = run(
        unpack_kernel,
        [summed, other],
        [
            shape((features, order), F32), shape((1, order), F32), shape((order, order), F32),
            shape((1, order), F32), shape((order, channels), F32),
        ],
        scratch=[pltpu.VMEM((2 * half, LANES), F32)],
    )
    return (
        gated[None], grad_one, bias_one.reshape(order), grad_two, bias_two.reshape(order),
        grad_three,
    )


def solution(mesh):
    return jax.shard_map(
        body,
        mesh=mesh,
        in_specs=(
            P("dp", "seq"),
            P(),
            P(),
            P(),
            P(),
            P(),
            P(),
            P(),
            P(),
            P(),
            P("dp", "seq", None),
        ),
        out_specs=(P("dp", "seq", None), P(), P(), P(), P(), P()),
        check_vma=False,
    )
```

```python
import functools
import math

import jax
import jax.numpy as jnp
import ml_dtypes
import numpy as np
from jax import lax
from jax.experimental import pallas as pl
from jax.experimental.pallas import tpu as pltpu
from jax.sharding import PartitionSpec as P

LETTERS = (65, 67, 71, 84, 97, 99, 103, 116, 78, 110)
GROUP = 16
LANES = 128
CHUNK = 8
SMALL = 24 * 1024 * 1024
LARGE = 56 * 1024 * 1024
F32 = jnp.float32
BF16 = jnp.bfloat16


def halves(table):
    high = table.astype(np.float32).astype(ml_dtypes.bfloat16)
    low = (table - high.astype(np.float64)).astype(np.float32).astype(ml_dtypes.bfloat16)
    return high, low


def band_numbers(length, band_count):
    return [
        max(band + 1, int(0.4 * length ** (band / (band_count - 1)))) for band in range(band_count)
    ]


@functools.cache
def feature_tables(length, band_count):
    numbers = np.array(band_numbers(length, band_count), np.int64)
    residue = (numbers[:, None] * np.arange(length, dtype=np.int64)[None, :]) % length
    angles = residue * (2.0 * math.pi / length)
    return np.concatenate(halves(np.concatenate([np.sin(angles), np.cos(angles)], axis=0)), axis=0)


@functools.cache
def transform_tables(rows):
    theta = np.pi * (np.arange(rows) + 0.5) / rows
    angles = np.arange(rows)[:, None] * theta[None, :]
    forward = np.concatenate([np.cos(angles), -np.sin(angles)], axis=1)
    high, low = halves(forward)
    first = np.concatenate([high, low, high], axis=0)
    inv_high, inv_low = halves(forward.T / rows)
    inverse = np.concatenate([inv_high, inv_low], axis=1)
    sign = np.broadcast_to(np.where(np.arange(rows) % 2 == 0, 1.0, -1.0), (8, rows))
    return first, inverse, sign.astype(np.float32)


@functools.cache
def letter_tables(lanes):
    code = np.full((lanes,), -1, np.int32)
    pick = np.zeros((lanes, lanes), np.float32)
    for row in range(6 * GROUP):
        if row % GROUP < len(LETTERS):
            code[row] = LETTERS[row % GROUP]
            pick[row, code[row]] = 1.0
    code = np.ascontiguousarray(np.broadcast_to(code[:, None], (lanes, lanes)))
    return code, pick.astype(ml_dtypes.bfloat16)


def split(x):
    high = x.astype(BF16)
    return high, (x - high.astype(F32)).astype(BF16)


def mm(a, b, ca=1, cb=0):
    return lax.dot_general(a, b, (((ca,), (cb,)), ((), ())), preferred_element_type=F32)


def left_mm(stack, high, low, cb=0):
    m = stack.shape[0] // 2
    both = mm(stack, high, cb=cb)
    return both[:m] + both[m:] + mm(stack[:m], low, cb=cb)


def sin_cos(x):
    turns = jnp.floor(x * (1.0 / math.pi) + 0.5)
    r = x - turns * 3.140625
    r = r - turns * 9.67653589793116e-4
    z = r * r
    s = -0.0001980613308286788 + z * 2.599125898339353e-06
    s = -0.16666656691981288 + z * (0.00833300936890471 + z * s)
    c = 2.476157712136818e-05 + z * -2.607203341358802e-07
    c = -0.49999999533050865 + z * (0.04166664015321537 + z * (-0.0013888396896628193 + z * c))
    half = turns * 0.5
    sign = 1.0 - 4.0 * (half - jnp.floor(half))
    return sign * (r + r * z * s), sign + (sign * z) * c


def forward(block, first_ref):
    high, low = split(block)
    return mm(jnp.concatenate([high, high, low], axis=1), first_ref[...])


def inverse(real, imag, inverse_ref):
    rows = real.shape[1]
    high, low = split(jnp.concatenate([real, imag], axis=1))
    both = mm(high, inverse_ref[...])
    return both[:, :rows] + both[:, rows:] + mm(low, inverse_ref[:, :rows])


def window_block(rates, start, rows, length):
    place = (lax.broadcasted_iota(jnp.int32, (1, rows), 1) + start).astype(F32) * (-1.0 / length)
    return jnp.exp(rates * place) * (1.0 / math.sqrt(length))


def window_step(rates, rows, length):
    return jnp.exp(rates * (-rows / length))


def column_stack(weights):
    return jnp.concatenate(split(weights.T), axis=0)


def row_stack(weights):
    high, low = split(weights.T)
    return jnp.concatenate([high, high, low], axis=1)


def layer(stack, values, bias):
    size = values.shape[0] // 2
    count = values.shape[1] // LANES
    column = jnp.broadcast_to(bias, (LANES, bias.shape[1])).T
    sine, cosine = sin_cos(
        left_mm(stack, values[:size], values[size:]) + jnp.concatenate([column] * count, axis=1)
    )
    return jnp.concatenate(split(sine), axis=0), cosine


def lookup_table(embed, taps, pick):
    chosen = mm(pick, embed)
    channels = taps.shape[2]
    pieces = []
    for branch in range(3):
        part = chosen[:, branch * channels : (branch + 1) * channels]
        scaled = [
            part[tap * GROUP : (tap + 1) * GROUP] * taps[branch, tap : tap + 1, :]
            for tap in range(3)
        ]
        high = jnp.concatenate(scaled, axis=0)
        rounded = high.astype(BF16).astype(F32)
        rest = jnp.zeros((LANES - 6 * GROUP, channels), F32)
        pieces.append(jnp.concatenate([rounded, high - rounded, rest], axis=0).T)
    return jnp.concatenate(pieces, axis=0).astype(BF16)


def one_hot(tok_ref, own, block, code):
    rows = tok_ref.shape[1]

    def row(j):
        got = tok_ref[pl.ds(jnp.maximum(j, 0) ^ own, 1), :]
        return jnp.where(j >= 0, got, 0)

    now = jnp.broadcast_to(row(block), (8, rows))
    before = jnp.broadcast_to(row(block - 1), (8, rows))
    lane = lax.broadcasted_iota(jnp.int32, (8, rows), 1)
    shifted = [now]
    for tap in (1, 2):
        shifted.append(
            jnp.where(lane < tap, pltpu.roll(before, tap, 1), pltpu.roll(now, tap, 1))
        )
    wide = [jnp.concatenate([s, s], axis=0) for s in shifted]
    rest = jnp.zeros((LANES - 6 * GROUP, rows), jnp.int32)
    spread = jnp.concatenate(wide + wide + [rest], axis=0)
    return jnp.where(spread == code, 1.0, 0.0).astype(BF16)


def fetch(sources, targets, sems):
    copies = []
    for m, (source, target) in enumerate(zip(sources, targets)):
        if source.shape != target.shape:
            source = source.at[pl.ds(0, target.shape[0]), :]
        copies.append(pltpu.make_async_copy(source, target, sems.at[m]))
    for copy in copies:
        copy.start()
    return copies


def first_kernel(w_one, b_one, feat, act_one, cos_one):
    act, cosine = layer(column_stack(w_one[...]), feat[...], b_one[...])
    act_one[...] = act
    cos_one[...] = cosine


def second_kernel(apart, w_two, b_two, w_three, *refs):
    two_back, three_back = refs[-4:-2] if not apart else refs
    two_back[...] = jnp.concatenate(split(w_two[...]), axis=0)
    three_back[...] = jnp.concatenate(split(w_three[...]), axis=0)
    if not apart:
        act, cosine = layer(column_stack(w_two[...]), refs[0][...], b_two[...])
        refs[-2][...] = act
        refs[-1][...] = cosine


def table_kernel(count, *refs):
    sources, targets = refs[:count], refs[count : 2 * count - 6]
    table, skip_col, rates_col, cot_t = refs[2 * count - 6 : 2 * count - 2]
    embed, taps, pick, skip, rates, cot = refs[2 * count - 2 : -1]
    copies = fetch(sources, (embed, taps, pick, skip, rates, cot, *targets), refs[-1])
    for copy in copies[:6]:
        copy.wait()
    channels = cot.shape[1]
    table[...] = lookup_table(embed[...], taps[...], pick[...])
    skip_col[...] = jnp.broadcast_to(skip[...], (LANES, channels)).T
    rates_col[...] = jnp.broadcast_to(rates[...], (LANES, channels)).T
    cot_t[...] = cot[...].astype(F32).T
    for copy in copies[6:]:
        copy.wait()


def filter_kernel(length, rates_col, act_two, w_three, first, spectra, window, step):
    order = act_two.shape[0] // 2
    three = row_stack(w_three[...])
    window[...] = window_block(rates_col[...], 0, LANES, length)
    step[...] = window_step(rates_col[...], LANES, length)
    for k in range(0, length // LANES, 2):
        pair = min(2, length // LANES - k)
        at = slice(k * LANES, (k + pair) * LANES)
        filt = mm(three, jnp.concatenate([act_two[:, at], act_two[:order, at]], axis=0))
        for m in range(pair):
            if k + m:
                window[...] *= step[...]
            spectra[k + m] = forward(filt[:, m * LANES : (m + 1) * LANES] * window[...], first)


def shifted_sum(spec, i, slots, signs):
    rows = signs.shape[1]
    real, imag = spec[i, :, :rows], spec[i, :, rows:]
    if i + 1 < slots:
        real = real - signs * spec[i + 1, :, rows:]
        imag = imag + signs * spec[i + 1, :, :rows]
    return real, imag


def main_kernel(length, apart, *refs):
    tok = refs[0]
    table, rates_col, cot_t, feat, first, inv, sign, code, two_back, three_back = refs[1:11]
    if apart:
        w_one, b_one, w_two, b_two, w_three = refs[11:16]
        one_t, two_t = column_stack(w_one[...]), column_stack(w_two[...])
        three_t = row_stack(w_three[...])
        keep, send, query_t, signal_t, mixed, spec = refs[16:22]
    else:
        one_all, cos_one, two_all, cos_two = refs[11:15]
        keep, send, query_t, signal_t, spec = refs[15:20]
    hot, slope_high, slope_low, packed, window, step = refs[-6:]
    blocks, rows = tok.shape
    channels = cot_t.shape[0]
    order = two_back.shape[1]
    count = min(blocks, CHUNK)
    chunks = blocks // count
    own = lax.axis_index("seq")
    bit = lax.axis_index("dp") % 2
    codes = code[...]
    signs = jnp.broadcast_to(sign[0:1, :], (channels, rows))

    step[...] = window_step(rates_col[...], rows, length)
    own_hot = one_hot(tok, own, own, codes)
    query = mm(table[:channels, :], own_hot)
    query_t[...] = query
    up = forward(cot_t[...] * query, first)
    up_real, up_imag = up[:, :rows], up[:, rows:]

    def chunk(base):
        static = isinstance(base, int)
        slots = count if static else count + 1
        lane0 = base * rows if static else pl.multiple_of(base * rows, rows * count)
        for i in range(slots):
            hot[:, i * rows : (i + 1) * rows] = one_hot(tok, own, own - base - i, codes)
        span = pl.ds(lane0, count * rows)
        if apart:
            act_one, cosine_one = layer(one_t, feat[:, span], b_one[...])
            act_two, cosine_two = layer(two_t, act_one, b_two[...])
        else:
            act_one, cosine_one, act_two, cosine_two = (
                r[:, span] for r in (one_all, cos_one, two_all, cos_two)
            )
        for i in range(0, slots, 2):
            pair = min(2, slots - i)
            both = mm(table[channels:, :], hot[:, i * rows : (i + pair) * rows])
            signals = both[:channels] * both[channels:]
            parts = [signals[:, m * rows : (m + 1) * rows] for m in range(pair)]
            if i == 0:
                if static:
                    signal_t[...] = parts[0]
                else:

                    @pl.when(base == 0)
                    def _():
                        signal_t[...] = parts[0]

            made = forward(jnp.concatenate(parts, axis=0), first)
            for m in range(pair):
                spec[i + m] = made[m * channels : (m + 1) * channels]
        for i in range(count):
            real, imag = shifted_sum(spec, i, slots, signs)
            if i == 0:
                window[...] = window_block(rates_col[...], lane0, rows, length)
            else:
                window[...] *= step[...]
            weight = window[...]
            if apart:
                at = slice(i * rows, (i + 1) * rows)
                filt = mm(three_t, jnp.concatenate([act_two[:, at], act_two[:order, at]], axis=0))
                got = forward(filt * weight, first)
                g_real, g_imag = got[:, :rows], got[:, rows:]
                mixed[:, :rows] += g_real * real - g_imag * imag
                mixed[:, rows:] += g_real * imag + g_imag * real
            lag = inverse(
                up_real * real + up_imag * imag, up_imag * real - up_real * imag, inv
            )
            high, low = split(lag * weight)
            slope_high[:, i * rows : (i + 1) * rows] = high
            slope_low[:, i * rows : (i + 1) * rows] = low

        def put(at, value):
            if static:
                packed[at : at + value.shape[0], :] = value
            else:
                packed[at : at + value.shape[0], :] += value

        slopes_high, slopes_low = slope_high[...], slope_low[...]
        grad_three = left_mm(act_two, slopes_high, slopes_low, cb=1)
        for slab in range(channels // LANES):
            put(slab * order, grad_three[:, slab * LANES : (slab + 1) * LANES])
        back_two = left_mm(three_back[...], slopes_high, slopes_low) * cosine_two
        two_split = split(back_two)
        back_one = left_mm(two_back[...], *two_split) * cosine_one
        one_split = split(back_one)
        grad_two = left_mm(act_one, *two_split, cb=1)
        grad_one = left_mm(feat[:, span], *one_split, cb=1)
        ones = jnp.ones((8, count * rows), BF16)
        at = channels // LANES * order
        put(at, grad_one)
        at = at + grad_one.shape[0]
        put(at, grad_two)
        at = at + order
        put(at, mm(ones, one_split[0], cb=1) + mm(ones, one_split[1], cb=1))
        put(at + 8, mm(ones, two_split[0], cb=1) + mm(ones, two_split[1], cb=1))
        at = at + 16
        if static and packed.shape[0] > at:
            packed[at:, :] = jnp.zeros((packed.shape[0] - at, LANES), F32)

    if chunks == 1:
        chunk(0)
    else:
        if apart:
            mixed[...] = jnp.zeros(mixed.shape, F32)
        packed[...] = jnp.zeros(packed.shape, F32)

        @pl.loop(0, chunks)
        def _(q):
            chunk(q * count)

    half = keep.shape[0]
    keep[...] = packed[pl.ds(pl.multiple_of(bit * half, 8), half), :]
    send[...] = packed[pl.ds(pl.multiple_of((1 - bit) * half, 8), half), :]


def gate_kernel(apart, *refs):
    query_t, signal_t, skip_col, inv, sign, *mix, out = refs
    rows = query_t.shape[1]
    if apart:
        total = [mix[0][:, :rows], mix[0][:, rows:]]
    else:
        spec, spectra = mix
        signs = jnp.broadcast_to(sign[0:1, :], query_t.shape)
        total = [jnp.zeros(query_t.shape, F32)] * 2
        for i in range(spec.shape[0]):
            real, imag = shifted_sum(spec, i, spec.shape[0], signs)
            g_real, g_imag = spectra[i, :, :rows], spectra[i, :, rows:]
            total[0] += g_real * real - g_imag * imag
            total[1] += g_real * imag + g_imag * real
    convolved = inverse(*total, inv)
    gated = query_t[...] * (convolved + skip_col[...] * signal_t[...])
    out[...] = gated.T.astype(BF16)


def unpack_kernel(mine, other, grad_one, bias_one, grad_two, bias_two, grad_three, whole):
    half = mine.shape[0]
    bit = lax.axis_index("dp") % 2
    whole[pl.ds(pl.multiple_of(bit * half, 8), half), :] = mine[...]
    whole[pl.ds(pl.multiple_of((1 - bit) * half, 8), half), :] = other[...]
    order = grad_three.shape[0]
    slabs = grad_three.shape[1] // LANES
    for slab in range(slabs):
        grad_three[:, slab * LANES : (slab + 1) * LANES] = whole[
            slab * order : (slab + 1) * order, :
        ]
    at = slabs * order
    features = grad_one.shape[0]
    grad_one[...] = whole[at : at + features, :]
    grad_two[...] = whole[at + features : at + features + order, :]
    at = at + features + order
    bias_one[...] = whole[at : at + 1, :]
    bias_two[...] = whole[at + 8 : at + 9, :]


def run(kernel, ins, outs, scratch=(), flops=0, far=False, limit=SMALL):
    moved = sum(math.prod(a.shape) * a.dtype.itemsize for a in list(ins) + list(outs))
    if far:
        ins = [pltpu.with_memory_space_constraint(a, pltpu.HBM) for a in ins]
    return pl.pallas_call(
        kernel,
        out_shape=tuple(outs),
        in_specs=[pl.BlockSpec(memory_space=pl.ANY if far else pltpu.VMEM)] * len(ins),
        out_specs=tuple(pl.BlockSpec(memory_space=pltpu.VMEM) for _ in outs),
        scratch_shapes=list(scratch),
        compiler_params=pltpu.CompilerParams(vmem_limit_bytes=limit),
        cost_estimate=pl.CostEstimate(flops=flops, bytes_accessed=moved, transcendentals=0),
    )(*ins)


def swap_with(block, axis, distance):
    size = lax.axis_size(axis)
    return lax.ppermute(block, axis, [(i, i ^ distance) for i in range(size)])


def all_rows(row, same_row):
    rows = jnp.concatenate([same_row, swap_with(row, "seq", 1)], axis=0)
    for step in range(1, lax.axis_size("seq").bit_length() - 1):
        rows = jnp.concatenate([rows, swap_with(rows, "seq", 1 << step)], axis=0)
    return rows


def all_added(block, first_beside, second_beside):
    steps = [("dp", 1 << i) for i in range(1, lax.axis_size("dp").bit_length() - 1)]
    steps += [("seq", 1 << i) for i in range(lax.axis_size("seq").bit_length() - 1)]
    cut = (block.shape[0] // 2 + 7) // 8 * 8
    parts = [block[:cut], block[cut:]]
    made = first_beside(block)
    turn = len(steps) // 2
    for s in range(len(steps)):
        moves = (steps[s], steps[(s + turn) % len(steps)])
        parts = [part + swap_with(part, *move) for part, move in zip(parts, moves)]
        if s == 0:
            parts[1], made = lax.optimization_barrier((parts[1], made))
            made = second_beside(made)
        if s == 1:
            parts[0], made = lax.optimization_barrier((parts[0], made))
    return jnp.concatenate(parts, axis=0), made


def body(tokens, embed, taps, skip, rates, w_one, b_one, w_two, b_two, w_three, cotangent):
    blocks = lax.axis_size("seq")
    rows = tokens.shape[1]
    channels = skip.shape[0]
    features, order = w_one.shape
    length = rows * blocks
    apart = blocks > CHUNK
    limit = LARGE if apart else SMALL
    shape = jax.ShapeDtypeStruct

    feat = jnp.asarray(feature_tables(length, features // 2))
    first, inv, sign = (jnp.asarray(t) for t in transform_tables(rows))
    code, pick = (jnp.asarray(t) for t in letter_tables(LANES))
    wide = (order, length)
    column = shape((channels, LANES), F32)
    held = [
        embed, taps, pick, skip.reshape(1, channels), rates.reshape(1, channels), cotangent[0],
        w_one, b_one.reshape(1, order), feat, w_two, b_two.reshape(1, order), w_three, tokens,
        first, inv, sign, code,
    ]
    shapes = [shape(a.shape, a.dtype) for a in held]
    shapes[0] = shape((LANES, embed.shape[1]), embed.dtype)
    near = run(
        functools.partial(table_kernel, len(held)),
        held,
        shapes[6:] + [shape((3 * channels, LANES), BF16), column, column, column],
        scratch=[pltpu.VMEM(a.shape, a.dtype) for a in shapes[:6]]
        + [pltpu.SemaphoreType.DMA((len(held),))],
        flops=5 * 10**8,
        far=True,
        limit=limit,
    )
    w_one, b_one, feat, w_two, b_two, w_three, own_tokens, first, inv, sign, code = near[:11]
    table, skip_col, rates_col, cot_t = near[11:]
    gathered = all_rows(tokens, own_tokens)
    act_one = []
    layer_outs = [] if apart else [shape((2 * order, length), BF16), shape(wide, F32)]
    if not apart:
        act_one = run(
            first_kernel, [w_one, b_one, feat], layer_outs, flops=5 * 10**8, limit=limit
        )
    two_back, three_back, *act_two = run(
        functools.partial(second_kernel, apart),
        [w_two, b_two, w_three, *act_one[:1]],
        [shape((2 * order, order), BF16), shape((2 * order, channels), BF16)] + layer_outs,
        flops=5 * 10**8,
        limit=limit,
    )

    total = channels // LANES * order + features + order + 16
    half = (total // 2 + 7) // 8 * 8
    count = min(blocks, CHUNK)
    slots = count if blocks == count else count + 1
    spec_shape = (slots, channels, 2 * rows)
    main_outs = [shape((half, LANES), F32)] * 2 + [shape((channels, rows), F32)] * 2
    scratch = [
        pltpu.VMEM((LANES, slots * rows), BF16),
        pltpu.VMEM((channels, count * rows), BF16),
        pltpu.VMEM((channels, count * rows), BF16),
        pltpu.VMEM((2 * half, LANES), F32),
        pltpu.VMEM((channels, rows), F32),
        pltpu.VMEM((channels, rows), F32),
    ]
    if apart:
        main_outs += [shape((channels, 2 * rows), F32)]
        scratch = [pltpu.VMEM(spec_shape, F32)] + scratch
    else:
        main_outs += [shape(spec_shape, F32)]
    main_ins = [gathered, table, rates_col, cot_t, feat, first, inv, sign, code, two_back]
    keep, send, query_t, signal_t, mix = run(
        functools.partial(main_kernel, length, apart),
        main_ins
        + [three_back]
        + ([w_one, b_one, w_two, b_two, w_three] if apart else [*act_one, *act_two]),
        main_outs,
        scratch=scratch,
        flops=6 * 10**9,
        limit=limit,
    )

    def first_beside(held_back):
        if apart:
            return ()
        act, _ = lax.optimization_barrier((act_two[0], held_back))
        return run(
            functools.partial(filter_kernel, length),
            [rates_col, act, w_three, first],
            [shape((blocks, channels, 2 * rows), F32)],
            scratch=[pltpu.VMEM((channels, LANES), F32)] * 2,
            flops=2 * 10**9,
            limit=limit,
        )

    def second_beside(spectra):
        (gated,) = run(
            functools.partial(gate_kernel, apart),
            [query_t, signal_t, skip_col, inv, sign, mix, *spectra],
            [shape((rows, channels), BF16)],
            flops=10**9,
            limit=limit,
        )
        return gated

    summed, gated = all_added(keep + swap_with(send, "dp", 1), first_beside, second_beside)
    other = swap_with(summed, "dp", 1)
    grad_one, bias_one, grad_two, bias_two, grad_three = run(
        unpack_kernel,
        [summed, other],
        [
            shape((features, order), F32), shape((1, order), F32), shape((order, order), F32),
            shape((1, order), F32), shape((order, channels), F32),
        ],
        scratch=[pltpu.VMEM((2 * half, LANES), F32)],
    )
    return (
        gated[None], grad_one, bias_one.reshape(order), grad_two, bias_two.reshape(order),
        grad_three,
    )


def solution(mesh):
    return jax.shard_map(
        body,
        mesh=mesh,
        in_specs=(
            P("dp", "seq"),
            P(),
            P(),
            P(),
            P(),
            P(),
            P(),
            P(),
            P(),
            P(),
            P("dp", "seq", None),
        ),
        out_specs=(P("dp", "seq", None), P(), P(), P(), P(), P()),
        check_vma=False,
    )
```
